32 devices in a mesh: section: 2 (over x), dp: 4 (over y, core), expert: 4 (over z).
Axes of the slice: x: 2, y: 2, z: 4, core: 2. Of those that a mesh axis runs over, the one named last changes fastest.
Arguments:
- inbound: bfloat16 [2, 16, 256, 1024], P('section', ('dp', 'expert')), may hold values from -6 to 6
- queued: bfloat16 [16, 256, 1024], P(('dp', 'expert')), may hold values from -6 to 6
- routes: int32 [2, 2, 16, 256, 1], P('section', None, ('dp', 'expert')), may hold values from 0 to 3
- first_gain: float32 [2, 1024], P('section'), may hold values from 0.1 to 1.9
- attention_in: bfloat16 [2, 1024, 1536], P('section', 'dp'), may hold values from -3.1875 to 3.1875
- attention_out: bfloat16 [2, 512, 1024], P('section', 'dp'), may hold values from -0.25 to 0.25
- second_gain: float32 [2, 1024], P('section'), may hold values from 0.1 to 1.9
- router: bfloat16 [2, 1024, 4], P('section'), may hold values from -0.375 to 0.375
- expert_in: bfloat16 [2, 4, 1024, 2048], P('section', 'expert', 'dp'), may hold values from -0.1875 to 0.1875
- expert_out: bfloat16 [2, 4, 2048, 1024], P('section', 'expert', 'dp'), may hold values from -0.125 to 0.125
Outputs:
- section_output: bfloat16 [2, 2, 16, 256, 1024], P('section', None, ('dp', 'expert'))
The draws below stay inside these ranges and needn't reach their ends.
All inputs are finite; a program needn't handle non-finite values.
Results may differ from the reference program's by a relative error of at most 0.0056.
Values may be sent and summed in bfloat16 or wider, within the bound.
A program may use at most 64 MiB of HBM per device.

```python
from functools import partial
import jax
import jax.numpy as jnp
from jax import lax

D = 1024
HEADS = 8
HEAD_DIM = 64
HID = 2048
SEQ = 256
CAP = 16
EXPERTS = 4
IMAGES = 16


def draw_attention_in(key, part):
    query_key, other_key, value_key = jax.random.split(key, 3)
    head_width = HEADS * HEAD_DIM
    scaling = 1.0 / jnp.sqrt(jnp.float32(D))
    normal_base = jax.random.truncated_normal(query_key, -4.0, 4.0, (2, D, head_width), jnp.float32)
    normal_other = jax.random.truncated_normal(other_key, -4.0, 4.0, (2, D, head_width), jnp.float32)
    queries = normal_base
    key_block = normal_other
    value_block = jax.random.truncated_normal(value_key, -4.0, 4.0, (2, D, head_width), jnp.float32)
    return (jnp.concatenate([queries, key_block, value_block], axis=2) * scaling).astype(jnp.bfloat16)


def block_levels(rng, dims, shards, smallest, high):
    loudness, own = 1.0, jax.random.fold_in(rng, 6)
    for dim, shards_of in shards:
        heights = jnp.exp(jax.random.uniform(jax.random.fold_in(own, dim), (shards_of,), jnp.float32, smallest / len(shards), high / len(shards)))
        loudness = loudness * jnp.repeat(heights, dims[dim] // shards_of).reshape([-1 if axis == dim else 1 for axis in range(len(dims))])
    return loudness


def choose_distinct(rng, rows, number_of, top, lift):
    order = jax.random.permutation(jax.random.fold_in(rng, 1), number_of)
    boost = order
    for power in range(3):
        boost = boost * boost // number_of
    boost = boost * lift // number_of
    tickets = jax.random.randint(jax.random.fold_in(rng, 2), (rows, number_of), 0, 4096) + boost
    sure = jax.random.permutation(jax.random.fold_in(rng, 3), rows)[jnp.arange(number_of) % rows]
    tickets = jnp.where(jnp.arange(rows)[:, None] == sure[None, :], 1 << 14, tickets)
    score = tickets * number_of + jnp.arange(number_of)
    return lax.top_k(score.astype(jnp.int32), top)[1].astype(jnp.int32)


def normal_values(stream_key, dims, deviation, most, pieces=(), held_as=jnp.bfloat16):
    entries = jax.random.normal(stream_key, dims, jnp.float32) * deviation
    if len(pieces) > 0:
        entries = block_levels(stream_key, dims, pieces, -0.22, 0.18) * entries
    return jnp.clip(entries, min=-most, max=most).astype(held_as)


def setup_inputs(seed: int = 0) -> dict:
    arg_keys = jax.random.split(jax.random.key(seed), 11)
    return {
        "inbound": normal_values(arg_keys[0], (2, IMAGES, SEQ, D), 1.0, 6.0, ((0, 2), (1, 16))),
        "queued": normal_values(arg_keys[1], (IMAGES, SEQ, D), 1.0, 6.0, ((0, 16),)),
        "routes": choose_distinct(arg_keys[2], 2 * 2 * IMAGES * SEQ, EXPERTS, 1, 2048).reshape((2, 2, IMAGES, SEQ, 1)),
        "first_gain": jnp.clip(1.0 + 0.18 * jax.random.normal(arg_keys[3], (2, D), jnp.float32), 0.1, 1.9),
        "attention_in": draw_attention_in(jax.random.fold_in(arg_keys[10], 71), 0),
        "attention_out": normal_values(arg_keys[5], (2, HEADS * HEAD_DIM, D), (HEADS * HEAD_DIM) ** -0.5, 0.25, ((0, 2), (1, 4))),
        "second_gain": jnp.clip(1.0 + 0.18 * jax.random.normal(arg_keys[6], (2, D), jnp.float32), 0.1, 1.9),
        "router": normal_values(arg_keys[7], (2, D, EXPERTS), (D // 4) ** -0.5, 0.375, ((0, 2),)),
        "expert_in": normal_values(arg_keys[8], (2, EXPERTS, D, HID), D ** -0.5, 0.1875, ((0, 2), (1, 4), (2, 4))),
        "expert_out": normal_values(arg_keys[9], (2, EXPERTS, HID, D), HID ** -0.5, 0.125, ((0, 2), (1, 4), (2, 4))),
    }


EPSILON = 1e-06

def layer_norm(activations, gain_vector):
    widened = activations.astype(jnp.float32)
    centre = widened - lax.optimization_barrier(jnp.mean(widened, axis=-1, keepdims=True))
    spread = lax.optimization_barrier(jnp.mean(centre * centre, axis=-1, keepdims=True))
    return (centre * lax.rsqrt(spread + EPSILON) * gain_vector).astype(jnp.bfloat16)

def build_slots(chosen, expert_count):
    onehot = (chosen[:, None] == jnp.arange(expert_count, dtype=jnp.int32)[None, :]).astype(jnp.int32)
    before = jnp.cumsum(onehot, axis=0) - onehot
    position = lax.optimization_barrier(jnp.sum(before * onehot, axis=1))
    retained = position < CAP
    slot_index = chosen * CAP + position
    slot_table = (slot_index[:, None] == jnp.arange(expert_count * CAP, dtype=jnp.int32)[None, :]) & retained[:, None]
    return (onehot, slot_table)

def attend_image(tokens, gain_vector, project_in, project_out):
    head_width = HEADS * HEAD_DIM
    normed = layer_norm(tokens, gain_vector)
    mixed_rows = jnp.dot(normed, project_in, preferred_element_type=jnp.float32).astype(jnp.bfloat16)
    queries = mixed_rows[:, :head_width].reshape(SEQ, HEADS, HEAD_DIM).astype(jnp.float32)
    key_rows = mixed_rows[:, head_width:2 * head_width].reshape(SEQ, HEADS, HEAD_DIM).astype(jnp.float32)
    value_rows = mixed_rows[:, 2 * head_width:].reshape(SEQ, HEADS, HEAD_DIM).astype(jnp.float32)
    scores = jnp.einsum('shd,thd->hst', queries, key_rows) * HEAD_DIM ** (-0.5)
    softmax_weights = jax.nn.softmax(scores, axis=-1).astype(jnp.bfloat16)
    context = jnp.einsum('hst,thd->shd', softmax_weights.astype(jnp.float32), value_rows)
    context = context.astype(jnp.bfloat16).reshape(SEQ, head_width)
    branch = jnp.dot(context, project_out, preferred_element_type=jnp.float32)
    return (tokens.astype(jnp.float32) + branch).astype(jnp.bfloat16)

def run_expert(operands):
    flat_rows, w_first, w_second = operands
    hidden = jax.nn.gelu(jnp.dot(flat_rows, w_first, preferred_element_type=jnp.float32), approximate=False).astype(jnp.bfloat16)
    return jnp.dot(hidden, w_second, preferred_element_type=jnp.float32).astype(jnp.bfloat16)

def layer(tokens, chosen, gain_one, project_in, project_out, gain_two, router_cols, expert_first, expert_second):
    residual = lax.map(lambda single: attend_image(single, gain_one, project_in, project_out), tokens)
    normed = layer_norm(residual, gain_two)
    logits = jnp.einsum('isd,de->ise', normed.astype(jnp.float32), router_cols.astype(jnp.float32))
    onehot, slot_table = jax.vmap(partial(build_slots, expert_count=EXPERTS))(chosen)
    gating = jax.nn.sigmoid(lax.optimization_barrier(jnp.sum(logits * onehot.astype(jnp.float32), axis=-1)))
    table_float = slot_table.astype(jnp.float32)
    outgoing = jnp.einsum('isk,isd->ikd', table_float, normed.astype(jnp.float32)).astype(jnp.bfloat16)
    outgoing = outgoing.reshape(IMAGES, EXPERTS, CAP, D).transpose(1, 0, 2, 3).reshape(EXPERTS, IMAGES * CAP, D)
    answered = lax.map(run_expert, (outgoing, expert_first, expert_second))
    answered = answered.reshape(EXPERTS, IMAGES, CAP, D).transpose(1, 0, 2, 3).reshape(IMAGES, EXPERTS * CAP, D)
    combined = jnp.einsum('isk,ikd->isd', table_float, answered.astype(jnp.float32))
    return (residual.astype(jnp.float32) + gating[:, :, None] * combined).astype(jnp.bfloat16)

def reference(inbound, queued, routes, first_gain, attention_in, attention_out, second_gain, router, expert_in, expert_out):

    def section_layer(section_index, tokens, tick_index):
        return layer(tokens, routes[section_index, tick_index, :, :, 0], first_gain[section_index], attention_in[section_index], attention_out[section_index], second_gain[section_index], router[section_index], expert_in[section_index], expert_out[section_index])
    first_early = section_layer(0, inbound[0], 0)
    second_early = section_layer(1, inbound[1], 0)
    first_later = section_layer(0, queued, 1)
    second_later = section_layer(1, first_early, 1)
    return jnp.stack([jnp.stack([first_early, first_later]), jnp.stack([second_early, second_later])])
```

```python
import functools

import jax
import jax.numpy as jnp
from jax import lax
from jax.experimental import pallas as pl
from jax.experimental.pallas import tpu as pltpu
from jax.sharding import PartitionSpec as P

HEAD_DIM = 64
CAP = 16
EPSILON = 1e-06
MESH = pl.DeviceIdType.MESH
F32, BF16 = jnp.float32, jnp.bfloat16
LANES = 128


def dot(a, b):
    return jnp.dot(a, b, preferred_element_type=F32)


def rows_of(start, size):
    return pl.ds(pl.multiple_of(start, 16), size)


def kernel(
    dp, ex, pieces,
    inbound, queued, routes, gain_a, att_in, att_out, gain_b, router, exp_in, exp_out,
    out,
    full_in, full_out, w1, normed, qkv, ctx, entering, mixed, table, table_t, onehot, gate, sent,
    rows, partial, parts, answer, answered, far_mixed, far_gate, far_ans, hid,
    own_sem, sib_s, sib_r, y_s, y_r, fz_s, fz_r, fs_s, fs_r, gs_s, gs_r, w_s, w_r,
    z1_s, z1_r, g_s, g_r, p_s, p_r, z2_s, z2_r, x_s, x_r,
):
    sec, d, e = lax.axis_index("section"), lax.axis_index("dp"), lax.axis_index("expert")
    y, c, half = d // 2, d % 2, e % 2
    ny = dp // 2
    sib, zpal, far = y * 2 + 1 - c, e + 1 - 2 * half, 1 - sec
    seq, width = inbound.shape
    k_rows = ex * CAP
    hid_own = w1.shape[1]
    heads_w = full_out.shape[0]
    in_rows, out_rows = att_in.shape[0], att_out.shape[0]

    def copy(src, dst, s_sem, r_sem, to):
        return pltpu.make_async_remote_copy(
            src_ref=src, dst_ref=dst, send_sem=s_sem, recv_sem=r_sem,
            device_id=to, device_id_type=MESH,
        )

    barrier = pltpu.get_barrier_semaphore()
    for k in range(1, dp):
        pl.semaphore_signal(barrier, inc=1, device_id={"dp": lax.rem(d + k, dp)}, device_id_type=MESH)
    for k in range(1, ex):
        pl.semaphore_signal(barrier, inc=1, device_id={"expert": lax.rem(e + k, ex)}, device_id_type=MESH)
    pl.semaphore_signal(barrier, inc=1, device_id={"section": far}, device_id_type=MESH)
    pl.semaphore_wait(barrier, dp + ex - 1)

    pending = []

    def send(*a):
        one = copy(*a)
        one.start()
        pending.append(one)

    leaving = []

    def leave(*a):
        one = copy(*a)
        one.start()
        leaving.append(one)

    weights = ((0, att_in, full_in, in_rows, pieces[0]), (1, att_out, full_out, out_rows, pieces[1]))
    chunk_list = []
    base = 0
    for which, src, dst, n, cuts in weights:
        size = n // 2 // cuts
        for i in range(cuts):
            chunk_list.append((base + i, src, dst, n, size, i))
        base += cuts
    for idx, src, dst, n, size, i in chunk_list:
        for k in range(1, ny):
            there = lax.rem(y + k, ny) * 2 + c
            off = half * (n // 2) + i * size
            send(src.at[rows_of(off, size)], dst.at[rows_of(d * n + off, size)],
                 y_s.at[idx, k - 1], y_r.at[idx, k - 1], {"dp": there})
    own = []
    for which, src, dst, n, cuts in weights:
        send(src, dst.at[rows_of(d * n, n)], sib_s.at[which], sib_r.at[which], {"dp": sib})
        here = pltpu.make_async_copy(src, dst.at[rows_of(d * n, n)], own_sem.at[which])
        here.start()
        own.append(here)
    w_rows = exp_in.shape[0]
    here = pltpu.make_async_copy(
        exp_in.at[:, pl.ds(pl.multiple_of(d * hid_own, LANES), hid_own)],
        w1.at[rows_of(d * w_rows, w_rows)], own_sem.at[2])
    here.start()
    own.append(here)

    lane = lax.broadcasted_iota(jnp.int32, (seq, LANES), 1)
    wide = table_t.shape[1]
    slots = lax.broadcasted_iota(jnp.int32, (seq, wide), 1)
    earlier = (lax.broadcasted_iota(jnp.int32, (seq, seq), 0)
               > lax.broadcasted_iota(jnp.int32, (seq, seq), 1)).astype(F32).astype(BF16)
    slot_of = []
    for t in range(2):
        chosen = routes[t]
        hot = (lane == chosen).astype(F32)
        place = jnp.sum(dot(earlier, hot.astype(BF16)) * hot, axis=1, keepdims=True)
        slot = jnp.where(place < CAP, chosen.astype(F32) * CAP + place, -1.0)
        full = (slots.astype(F32) == slot).astype(F32)
        table[t] = full[:, :k_rows].astype(BF16)
        table_t[t] = full.T.astype(BF16)
        onehot[t] = hot
        slot_of.append(slot)

    def norm(src, gain):
        step = 32

        def body(i, _):
            at = pl.ds(pl.multiple_of(i * step, step), step)
            v = src[at, :].astype(F32)
            centre = v - jnp.mean(v, axis=-1, keepdims=True)
            spread = jnp.mean(centre * centre, axis=-1, keepdims=True)
            normed[at, :] = (centre * lax.rsqrt(spread + EPSILON) * gain[...]).astype(BF16)
            return 0

        lax.fori_loop(0, seq // step, body, 0)

    norm(inbound, gain_a)

    for idx, src, dst, n, size, i in chunk_list:
        for k in range(1, ny):
            come = lax.rem(y - k + ny, ny) * 2 + c
            view = dst.at[rows_of(come * n + half * (n // 2) + i * size, size)]
            copy(view, view, y_s.at[idx, k - 1], y_r.at[idx, k - 1], {"dp": come}).wait_recv()
            send(view, view, fz_s.at[idx, k - 1], fz_r.at[idx, k - 1], {"expert": zpal})
            send(view, view, fs_s.at[idx, k - 1], fs_r.at[idx, k - 1], {"dp": sib})
    for k in range(1, dp):
        to = lax.rem(d + k, dp)
        send(exp_in.at[:, pl.ds(pl.multiple_of(to * hid_own, LANES), hid_own)],
             w1.at[rows_of(d * w_rows, w_rows)], w_s.at[k - 1], w_r.at[k - 1], {"dp": to})
    for idx, src, dst, n, size, i in chunk_list:
        for k in range(1, ny):
            come = lax.rem(y - k + ny, ny) * 2 + c
            view = dst.at[rows_of(come * n + (1 - half) * (n // 2) + i * size, size)]
            copy(view, view, fz_s.at[idx, k - 1], fz_r.at[idx, k - 1], {"expert": zpal}).wait_recv()
            send(view, view, gs_s.at[idx, k - 1], gs_r.at[idx, k - 1], {"dp": sib})

    def land(which):
        _, src, dst, n, cuts = weights[which]
        own[which].wait()
        view = dst.at[rows_of(sib * n, n)]
        copy(view, view, sib_s.at[which], sib_r.at[which], {"dp": sib}).wait_recv()
        for idx, _, to, n, size, i in chunk_list:
            if to is not dst:
                continue
            for k in range(1, ny):
                come = lax.rem(y - k + ny, ny) * 2 + 1 - c
                view = dst.at[rows_of(come * n + half * (n // 2) + i * size, size)]
                copy(view, view, fs_s.at[idx, k - 1], fs_r.at[idx, k - 1], {"dp": sib}).wait_recv()
                view = dst.at[rows_of(come * n + (1 - half) * (n // 2) + i * size, size)]
                copy(view, view, gs_s.at[idx, k - 1], gs_r.at[idx, k - 1], {"dp": sib}).wait_recv()

    low = lax.broadcasted_iota(jnp.int32, (seq, LANES), 1) < HEAD_DIM

    for t in range(2):
        if t == 0:
            source = inbound
            land(0)
        else:
            source = entering
            for i, view in enumerate((far_mixed, far_gate, far_ans)):
                copy(view, view, x_s.at[i], x_r.at[i], {"section": far}).wait_recv()
            far_table = (slots.astype(F32) == far_gate[:, 1:2]).astype(F32)[:, :k_rows].astype(BF16)
            for j in range(0, width, 256):
                at = slice(j, j + 256)
                came = (far_mixed[:, at].astype(F32)
                        + far_gate[:, 0:1] * dot(far_table, far_ans[:, at]))
                entering[:, at] = jnp.where(sec == 0, queued[:, at].astype(F32), came).astype(BF16)
            norm(entering, gain_a)
        for j in range(0, 3 * heads_w, 256):
            qkv[:, j:j + 256] = dot(normed[...], full_in[:, j:j + 256]).astype(BF16)
        for j in range(0, heads_w, LANES):
            q = qkv[:, j:j + LANES] * jnp.asarray(HEAD_DIM ** -0.5, BF16)
            key = qkv[:, heads_w + j:heads_w + j + LANES]
            val = qkv[:, 2 * heads_w + j:2 * heads_w + j + LANES]
            both = []
            for mask in (low, jnp.logical_not(low)):
                one = jnp.where(mask, q.astype(F32), 0.0).astype(BF16)
                s = lax.dot_general(one, key, (((1,), (1,)), ((), ())), preferred_element_type=F32)
                w = jnp.exp(s - jnp.max(s, axis=1, keepdims=True))
                both.append(dot(w.astype(BF16), val) / jnp.sum(w, axis=1, keepdims=True))
            ctx[:, j:j + LANES] = jnp.where(low, both[0], both[1]).astype(BF16)
        if t == 0:
            land(1)
        for j in range(0, width, 256):
            at = slice(j, j + 256)
            mixed[t, :, at] = (source[:, at].astype(F32) + dot(ctx[...], full_out[:, at])).astype(BF16)
        if t == 0:
            send(mixed.at[0], far_mixed, x_s.at[0], x_r.at[0], {"section": far})
        norm(mixed.at[t], gain_b)
        for j in range(0, width, 256):
            at = slice(j, j + 256)
            sent[t, :, at] = dot(table_t[t], normed[:, at])[:].astype(BF16)
        for k in range(1, ex):
            to = lax.rem(e + k, ex)
            send(sent.at[t, rows_of(to * CAP, CAP)], rows.at[t, d, rows_of(e * CAP, CAP)],
                 z1_s.at[t, k - 1], z1_r.at[t, k - 1], {"expert": to})
        rows[t, d, rows_of(e * CAP, CAP), :] = sent[t, rows_of(e * CAP, CAP), :]
        logits = dot(normed[...], router[...])
        picked = jnp.sum(logits * onehot[t][:, :ex], axis=1, keepdims=True)
        gating = 1.0 / (1.0 + jnp.exp(-picked))
        gate[t] = jnp.where(lane == 0, gating, jnp.where(lane == 1, slot_of[t], 0.0))
        if t == 0:
            send(gate.at[0], far_gate, x_s.at[1], x_r.at[1], {"section": far})
        for k in range(1, ex):
            come = lax.rem(e - k + ex, ex)
            view = rows.at[t, d, rows_of(come * CAP, CAP)]
            copy(view, view, z1_s.at[t, k - 1], z1_r.at[t, k - 1], {"expert": come}).wait_recv()
        for k in range(1, dp):
            send(rows.at[t, d], rows.at[t, d], g_s.at[t, k - 1], g_r.at[t, k - 1],
                 {"dp": lax.rem(d + k, dp)})
        if t == 0:
            own[2].wait()
            for k in range(1, dp):
                come = lax.rem(d - k + dp, dp)
                view = w1.at[rows_of(come * w_rows, w_rows)]
                copy(view, view, w_s.at[k - 1], w_r.at[k - 1], {"dp": come}).wait_recv()
        for k in range(1, dp):
            come = lax.rem(d - k + dp, dp)
            view = rows.at[t, come]
            copy(view, view, g_s.at[t, k - 1], g_r.at[t, k - 1], {"dp": come}).wait_recv()

        group = 4

        def experts(i, _):
            at = pl.ds(i * group, group)
            x = rows[t, at].reshape(group * k_rows, width)
            for j in range(0, hid_own, 128):
                h = dot(x, w1[:, j:j + 128])
                h = 0.5 * h * (1.0 + lax.erf(h * 0.7071067811865476))
                hid[:, j:j + 128] = h.astype(BF16)
            for j in range(0, width, 256):
                a = dot(hid[...], exp_out[:, j:j + 256]).astype(BF16)
                partial[at, :, j:j + 256] = a.reshape(group, k_rows, 256)
            return 0

        for one in leaving:
            one.wait_send()
        leaving.clear()
        lax.fori_loop(0, dp // group, experts, 0)
        for k in range(1, dp):
            to = lax.rem(d + k, dp)
            leave(partial.at[to], parts.at[t, k - 1], p_s.at[t, k - 1], p_r.at[t, k - 1], {"dp": to})
        for k in range(1, dp):
            come = lax.rem(d - k + dp, dp)
            view = parts.at[t, k - 1]
            copy(view, view, p_s.at[t, k - 1], p_r.at[t, k - 1], {"dp": come}).wait_recv()
        for i in range(ex):
            at = slice(i * CAP, i * CAP + CAP)
            total = partial[d, at, :].astype(F32)
            for k in range(1, dp):
                total += parts[t, k - 1, at, :].astype(F32)
            answer[t, at, :] = total.astype(BF16)
        for k in range(1, ex):
            to = lax.rem(e + k, ex)
            send(answer.at[t, rows_of(to * CAP, CAP)], answered.at[t, rows_of(e * CAP, CAP)],
                 z2_s.at[t, k - 1], z2_r.at[t, k - 1], {"expert": to})
        answered[t, rows_of(e * CAP, CAP), :] = answer[t, rows_of(e * CAP, CAP), :]
        for k in range(1, ex):
            come = lax.rem(e - k + ex, ex)
            view = answered.at[t, rows_of(come * CAP, CAP)]
            copy(view, view, z2_s.at[t, k - 1], z2_r.at[t, k - 1], {"expert": come}).wait_recv()
        if t == 0:
            send(answered.at[0], far_ans, x_s.at[2], x_r.at[2], {"section": far})
        for j in range(0, width, 256):
            at = slice(j, j + 256)
            out[t, :, at] = (mixed[t, :, at].astype(F32)
                             + gate[t][:, 0:1] * dot(table[t], answered[t, :, at])).astype(BF16)
    for one in pending + leaving:
        one.wait_send()


def per_device(dp, ex, inbound, queued, routes, gain_a, att_in, att_out, gain_b, router, exp_in, exp_out):
    seq, width = queued.shape[1:]
    k_rows = ex * CAP
    wide = max(k_rows, LANES)
    hid_own = exp_out.shape[2]
    heads_w = att_out.shape[1] * dp
    cols = att_in.shape[2]
    in_rows, out_rows = att_in.shape[1], att_out.shape[1]
    pieces = (max(1, min(4, in_rows // 32)), max(1, min(2, out_rows // 32)))
    n, ny = sum(pieces), max(dp // 2 - 1, 1)
    vm, dma = pltpu.VMEM, pltpu.SemaphoreType.DMA
    scratch = [
        vm((width, cols), BF16), vm((heads_w, width), BF16), vm((width, hid_own), BF16),
        vm((seq, width), BF16), vm((seq, cols), BF16), vm((seq, heads_w), BF16),
        vm((seq, width), BF16), vm((2, seq, width), BF16), vm((2, seq, k_rows), BF16),
        vm((2, wide, seq), BF16), vm((2, seq, LANES), F32), vm((2, seq, LANES), F32),
        vm((2, wide, width), BF16),
        vm((2, dp, k_rows, width), BF16), vm((dp, k_rows, width), BF16),
        vm((2, dp - 1, k_rows, width), BF16),
        vm((2, k_rows, width), BF16), vm((2, k_rows, width), BF16),
        vm((seq, width), BF16), vm((seq, LANES), F32), vm((k_rows, width), BF16),
        vm((4 * k_rows, hid_own), BF16),
        dma((3,)), dma((2,)), dma((2,)),
        *[dma((n, ny))] * 8,
        dma((dp - 1,)), dma((dp - 1,)),
        dma((2, ex - 1)), dma((2, ex - 1)), dma((2, dp - 1)), dma((2, dp - 1)),
        dma((2, dp - 1)), dma((2, dp - 1)), dma((2, ex - 1)), dma((2, ex - 1)),
        dma((3,)), dma((3,)),
    ]
    result = pl.pallas_call(
        functools.partial(kernel, dp, ex, pieces),
        out_shape=jax.ShapeDtypeStruct((2, seq, width), BF16),
        in_specs=[pl.BlockSpec(memory_space=pltpu.VMEM)] * 10,
        out_specs=pl.BlockSpec(memory_space=pltpu.VMEM),
        scratch_shapes=scratch,
        compiler_params=pltpu.CompilerParams(
            collective_id=0, has_side_effects=True, vmem_limit_bytes=60 * 2**20
        ),
    )(
        inbound[0, 0], queued[0], routes[0, :, 0], gain_a, att_in[0], att_out[0], gain_b,
        router[0], exp_in[0, 0], exp_out[0, 0],
    )
    return result[None, :, None]


def solution(mesh):
    in_specs = (
        P("section", ("dp", "expert"), None, None),
        P(("dp", "expert"), None, None),
        P("section", None, ("dp", "expert"), None, None),
        P("section", None),
        P("section", "dp", None),
        P("section", "dp", None),
        P("section", None),
        P("section", None, None),
        P("section", "expert", "dp", None),
        P("section", "expert", "dp", None),
    )
    out_specs = P("section", None, ("dp", "expert"), None, None)
    return jax.shard_map(
        functools.partial(per_device, mesh.shape["dp"], mesh.shape["expert"]),
        mesh=mesh, in_specs=in_specs, out_specs=out_specs, check_vma=False,
    )
```

```python
import functools

import jax
import jax.numpy as jnp
from jax import lax
from jax.experimental import pallas as pl
from jax.experimental.pallas import tpu as pltpu
from jax.sharding import PartitionSpec as P

HEAD_DIM = 64
CAP = 16
EPSILON = 1e-06
MESH = pl.DeviceIdType.MESH
F32, BF16 = jnp.float32, jnp.bfloat16
LANES = 128


def dot(a, b):
    return jnp.dot(a, b, preferred_element_type=F32)


def rows_of(start, size):
    return pl.ds(pl.multiple_of(start, 16), size)


def kernel(
    dp, ex, pieces,
    inbound_h, queued_h, routes, gain_a, att_in, att_out, gain_b, router, exp_in, exp_out_h,
    out_h,
    inbound, queued, exp_out, out,
    full_in, full_out, w1, normed, qkv, ctx, entering, mixed, table, table_t, onehot, gate, sent,
    rows, partial, near, parts, answer, answered, far_mixed, far_gate, far_ans, hid,
    own_sem, load_sem, save_sem, sib_s, sib_r, y_s, y_r, fz_s, fz_r, fs_s, fs_r, gs_s, gs_r, w_s, w_r,
    z1_s, z1_r, g_s, g_r, h_s, h_r, n_s, n_r, p_s, p_r, z2_s, z2_r, x_s, x_r,
):
    sec, d, e = lax.axis_index("section"), lax.axis_index("dp"), lax.axis_index("expert")
    y, c, half = d // 2, d % 2, e % 2
    ny = dp // 2
    sib, zpal, far = y * 2 + 1 - c, e + 1 - 2 * half, 1 - sec
    seq, width = inbound.shape
    k_rows = ex * CAP
    hid_own = w1.shape[1]
    heads_w = full_out.shape[0]
    in_rows, out_rows = att_in.shape[0], att_out.shape[0]

    def copy(src, dst, s_sem, r_sem, to):
        return pltpu.make_async_remote_copy(
            src_ref=src, dst_ref=dst, send_sem=s_sem, recv_sem=r_sem,
            device_id=to, device_id_type=MESH,
        )

    loads = []
    for i, (a, b) in enumerate(((inbound_h, inbound), (queued_h, queued), (exp_out_h, exp_out))):
        loads.append(pltpu.make_async_copy(a, b, load_sem.at[i]))
    loads[0].start()
    barrier = pltpu.get_barrier_semaphore()
    for k in range(1, dp):
        pl.semaphore_signal(barrier, inc=1, device_id={"dp": lax.rem(d + k, dp)}, device_id_type=MESH)
    for k in range(1, ex):
        pl.semaphore_signal(barrier, inc=1, device_id={"expert": lax.rem(e + k, ex)}, device_id_type=MESH)
    pl.semaphore_signal(barrier, inc=1, device_id={"section": far}, device_id_type=MESH)
    pl.semaphore_wait(barrier, dp + ex - 1)

    pending = []

    def send(*a):
        one = copy(*a)
        one.start()
        pending.append(one)

    leaving = []

    def leave(*a):
        one = copy(*a)
        one.start()
        leaving.append(one)

    weights = ((0, att_in, full_in, in_rows, pieces[0]), (1, att_out, full_out, out_rows, pieces[1]))
    chunk_list = []
    base = 0
    for which, src, dst, n, cuts in weights:
        size = n // 2 // cuts
        for i in range(cuts):
            chunk_list.append((base + i, src, dst, n, size, i))
        base += cuts
    for idx, src, dst, n, size, i in chunk_list:
        for k in range(1, ny):
            there = lax.rem(y + k, ny) * 2 + c
            off = half * (n // 2) + i * size
            send(src.at[rows_of(off, size)], dst.at[rows_of(d * n + off, size)],
                 y_s.at[idx, k - 1], y_r.at[idx, k - 1], {"dp": there})
    own = []
    for which, src, dst, n, cuts in weights:
        send(src, dst.at[rows_of(d * n, n)], sib_s.at[which], sib_r.at[which], {"dp": sib})
        here = pltpu.make_async_copy(src, dst.at[rows_of(d * n, n)], own_sem.at[which])
        here.start()
        own.append(here)
    w_rows = exp_in.shape[0]
    here = pltpu.make_async_copy(
        exp_in.at[:, pl.ds(pl.multiple_of(d * hid_own, LANES), hid_own)],
        w1.at[rows_of(d * w_rows, w_rows)], own_sem.at[2])
    here.start()
    own.append(here)

    loads[1].start()
    loads[2].start()

    lane = lax.broadcasted_iota(jnp.int32, (seq, LANES), 1)
    wide = table_t.shape[1]
    slots = lax.broadcasted_iota(jnp.int32, (seq, wide), 1)
    earlier = (lax.broadcasted_iota(jnp.int32, (seq, seq), 0)
               > lax.broadcasted_iota(jnp.int32, (seq, seq), 1)).astype(F32).astype(BF16)
    slot_of = []
    for t in range(2):
        chosen = jnp.broadcast_to(routes[t:t + 1, :].astype(F32), (LANES, seq)).T
        hot = (lane.astype(F32) == chosen).astype(F32)
        place = jnp.sum(dot(earlier, hot.astype(BF16)) * hot, axis=1, keepdims=True)
        slot = jnp.where(place < CAP, chosen[:, :1] * CAP + place, -1.0)
        full = (slots.astype(F32) == slot).astype(F32)
        table[t] = full[:, :k_rows].astype(BF16)
        table_t[t] = full.T.astype(BF16)
        onehot[t] = hot
        slot_of.append(slot)

    def norm(src, gain):
        step = 32

        def body(i, _):
            at = pl.ds(pl.multiple_of(i * step, step), step)
            v = src[at, :].astype(F32)
            centre = v - jnp.mean(v, axis=-1, keepdims=True)
            spread = jnp.mean(centre * centre, axis=-1, keepdims=True)
            normed[at, :] = (centre * lax.rsqrt(spread + EPSILON) * gain[...]).astype(BF16)
            return 0

        lax.fori_loop(0, seq // step, body, 0, unroll=True)

    loads[0].wait()
    norm(inbound, gain_a)

    for idx, src, dst, n, size, i in chunk_list:
        for k in range(1, ny):
            come = lax.rem(y - k + ny, ny) * 2 + c
            view = dst.at[rows_of(come * n + half * (n // 2) + i * size, size)]
            copy(view, view, y_s.at[idx, k - 1], y_r.at[idx, k - 1], {"dp": come}).wait_recv()
            send(view, view, fz_s.at[idx, k - 1], fz_r.at[idx, k - 1], {"expert": zpal})
            send(view, view, fs_s.at[idx, k - 1], fs_r.at[idx, k - 1], {"dp": sib})
    for k in range(1, dp):
        to = lax.rem(d + k, dp)
        send(exp_in.at[:, pl.ds(pl.multiple_of(to * hid_own, LANES), hid_own)],
             w1.at[rows_of(d * w_rows, w_rows)], w_s.at[k - 1], w_r.at[k - 1], {"dp": to})
    for idx, src, dst, n, size, i in chunk_list:
        for k in range(1, ny):
            come = lax.rem(y - k + ny, ny) * 2 + c
            view = dst.at[rows_of(come * n + (1 - half) * (n // 2) + i * size, size)]
            copy(view, view, fz_s.at[idx, k - 1], fz_r.at[idx, k - 1], {"expert": zpal}).wait_recv()
            send(view, view, gs_s.at[idx, k - 1], gs_r.at[idx, k - 1], {"dp": sib})

    def land(which):
        _, src, dst, n, cuts = weights[which]
        own[which].wait()
        view = dst.at[rows_of(sib * n, n)]
        copy(view, view, sib_s.at[which], sib_r.at[which], {"dp": sib}).wait_recv()
        for idx, _, to, n, size, i in chunk_list:
            if to is not dst:
                continue
            for k in range(1, ny):
                come = lax.rem(y - k + ny, ny) * 2 + 1 - c
                view = dst.at[rows_of(come * n + half * (n // 2) + i * size, size)]
                copy(view, view, fs_s.at[idx, k - 1], fs_r.at[idx, k - 1], {"dp": sib}).wait_recv()
                view = dst.at[rows_of(come * n + (1 - half) * (n // 2) + i * size, size)]
                copy(view, view, gs_s.at[idx, k - 1], gs_r.at[idx, k - 1], {"dp": sib}).wait_recv()

    far_views = [far_mixed, far_gate]
    for k in range(ex):
        far_views.append(far_ans.at[rows_of(lax.rem(e - k + ex, ex) * CAP, CAP)])
    low = lax.broadcasted_iota(jnp.int32, (seq, LANES), 1) < HEAD_DIM

    saves = []
    for t in range(2):
        if t == 0:
            source = inbound
            land(0)
        else:
            source = entering
            loads[1].wait()
            for i, view in enumerate(far_views):
                copy(view, view, x_s.at[i], x_r.at[i], {"section": far}).wait_recv()
            far_table = (slots.astype(F32) == far_gate[:, 1:2]).astype(F32)[:, :k_rows].astype(BF16)
            for j in range(0, width, 256):
                at = slice(j, j + 256)
                came = (far_mixed[:, at].astype(F32)
                        + far_gate[:, 0:1] * dot(far_table, far_ans[:, at]))
                entering[:, at] = jnp.where(sec == 0, queued[:, at].astype(F32), came).astype(BF16)
            norm(entering, gain_a)
        for j in range(0, 3 * heads_w, 256):
            qkv[:, j:j + 256] = dot(normed[...], full_in[:, j:j + 256]).astype(BF16)
        for j in range(0, heads_w, LANES):
            q = qkv[:, j:j + LANES] * jnp.asarray(HEAD_DIM ** -0.5, BF16)
            key = qkv[:, heads_w + j:heads_w + j + LANES]
            val = qkv[:, 2 * heads_w + j:2 * heads_w + j + LANES]
            both = []
            for mask in (low, jnp.logical_not(low)):
                one = jnp.where(mask, q.astype(F32), 0.0).astype(BF16)
                s = lax.dot_general(one, key, (((1,), (1,)), ((), ())), preferred_element_type=F32)
                w = jnp.exp(s - jnp.max(s, axis=1, keepdims=True))
                both.append(dot(w.astype(BF16), val) / jnp.sum(w, axis=1, keepdims=True))
            ctx[:, j:j + LANES] = jnp.where(low, both[0], both[1]).astype(BF16)
        if t == 0:
            land(1)
        for j in range(0, width, 256):
            at = slice(j, j + 256)
            mixed[t, :, at] = (source[:, at].astype(F32) + dot(ctx[...], full_out[:, at])).astype(BF16)
        if t == 0:
            send(mixed.at[0], far_mixed, x_s.at[0], x_r.at[0], {"section": far})
        norm(mixed.at[t], gain_b)
        for j in range(0, width, 256):
            at = slice(j, j + 256)
            sent[t, :, at] = dot(table_t[t], normed[:, at])[:].astype(BF16)
        for k in range(1, ex):
            to = lax.rem(e + k, ex)
            send(sent.at[t, rows_of(to * CAP, CAP)], rows.at[t, d, rows_of(e * CAP, CAP)],
                 z1_s.at[t, k - 1], z1_r.at[t, k - 1], {"expert": to})
        rows[t, d, rows_of(e * CAP, CAP), :] = sent[t, rows_of(e * CAP, CAP), :]
        logits = lax.dot_general(normed[...], router[...], (((1,), (1,)), ((), ())), preferred_element_type=F32)
        picked = jnp.sum(logits * onehot[t][:, :ex], axis=1, keepdims=True)
        gating = 1.0 / (1.0 + jnp.exp(-picked))
        gate[t] = jnp.where(lane == 0, gating, jnp.where(lane == 1, slot_of[t], 0.0))
        if t == 0:
            send(gate.at[0], far_gate, x_s.at[1], x_r.at[1], {"section": far})
        def pass_on(kk):
            at = rows_of(lax.rem(e - kk + ex, ex) * CAP, CAP)
            for k in range(1, ny):
                come = lax.rem(y - k + ny, ny) * 2 + c
                view = rows.at[t, come, at]
                copy(view, view, g_s.at[t, kk, k - 1], g_r.at[t, kk, k - 1], {"dp": come}).wait_recv()
                send(view, view, h_s.at[t, kk, k], h_r.at[t, kk, k], {"dp": sib})

        for kk in range(ex):
            come = lax.rem(e - kk + ex, ex)
            view = rows.at[t, d, rows_of(come * CAP, CAP)]
            if kk > 0:
                copy(view, view, z1_s.at[t, kk - 1], z1_r.at[t, kk - 1], {"expert": come}).wait_recv()
            for k in range(1, ny):
                send(view, view, g_s.at[t, kk, k - 1], g_r.at[t, kk, k - 1],
                     {"dp": lax.rem(y + k, ny) * 2 + c})
            send(view, view, h_s.at[t, kk, 0], h_r.at[t, kk, 0], {"dp": sib})
            if kk > 0:
                pass_on(kk - 1)
        pass_on(ex - 1)
        if t == 0:
            own[2].wait()
            loads[2].wait()
            for k in range(1, dp):
                come = lax.rem(d - k + dp, dp)
                view = w1.at[rows_of(come * w_rows, w_rows)]
                copy(view, view, w_s.at[k - 1], w_r.at[k - 1], {"dp": come}).wait_recv()
        for kk in range(ex):
            at = rows_of(lax.rem(e - kk + ex, ex) * CAP, CAP)
            for k in range(ny):
                view = rows.at[t, lax.rem(y - k + ny, ny) * 2 + 1 - c, at]
                copy(view, view, h_s.at[t, kk, k], h_r.at[t, kk, k], {"dp": sib}).wait_recv()

        group = 4

        def experts(i, _):
            at = pl.ds(i * group, group)
            x = rows[t, at].reshape(group * k_rows, width)
            for j in range(0, hid_own, 128):
                h = dot(x, w1[:, j:j + 128])
                h = 0.5 * h * (1.0 + lax.erf(h * 0.7071067811865476))
                hid[:, j:j + 128] = h.astype(BF16)
            for j in range(0, width, 256):
                a = dot(hid[...], exp_out[:, j:j + 256]).astype(BF16)
                partial[at, :, j:j + 256] = a.reshape(group, k_rows, 256)
            return 0

        for one in leaving:
            one.wait_send()
        leaving.clear()
        lax.fori_loop(0, dp // group, experts, 0)
        for k in (*range(1, ny), 0):
            to = lax.rem(y + k, ny) * 2
            leave(partial.at[to + 1 - c], near.at[t, k], n_s.at[t, k], n_r.at[t, k], {"dp": sib})
        for k in range(1, ny):
            to = lax.rem(y + k, ny) * 2 + c
            view = near.at[t, k]
            copy(view, view, n_s.at[t, k], n_r.at[t, k], {"dp": sib}).wait_recv()
            for kk in (*range(1, ex), 0):
                at = rows_of(lax.rem(e + kk, ex) * CAP, CAP)
                partial[to, at, :] = (partial[to, at, :].astype(F32) + near[t, k, at, :].astype(F32)).astype(BF16)
                leave(partial.at[to, at], parts.at[t, k - 1, at],
                      p_s.at[t, kk, k - 1], p_r.at[t, kk, k - 1], {"dp": to})
        view = near.at[t, 0]
        copy(view, view, n_s.at[t, 0], n_r.at[t, 0], {"dp": sib}).wait_recv()
        for kk in (*range(1, ex), 0):
            to = lax.rem(e + kk, ex)
            at = rows_of(to * CAP, CAP)
            total = partial[d, at, :].astype(F32) + near[t, 0, at, :].astype(F32)
            for k in range(1, ny):
                view = parts.at[t, k - 1, at]
                copy(view, view, p_s.at[t, kk, k - 1], p_r.at[t, kk, k - 1],
                     {"dp": lax.rem(y - k + ny, ny) * 2 + c}).wait_recv()
                total += parts[t, k - 1, at, :].astype(F32)
            if kk > 0:
                answer[t, at, :] = total.astype(BF16)
                send(answer.at[t, at], answered.at[t, rows_of(e * CAP, CAP)],
                     z2_s.at[t, kk - 1], z2_r.at[t, kk - 1], {"expert": to})
            else:
                answered[t, at, :] = total.astype(BF16)
        for kk in range(ex):
            come = lax.rem(e - kk + ex, ex)
            view = answered.at[t, rows_of(come * CAP, CAP)]
            if kk > 0:
                copy(view, view, z2_s.at[t, kk - 1], z2_r.at[t, kk - 1], {"expert": come}).wait_recv()
            if t == 0:
                send(view, far_views[2 + kk], x_s.at[2 + kk], x_r.at[2 + kk], {"section": far})
        for j in range(0, width, 256):
            at = slice(j, j + 256)
            out[t, :, at] = (mixed[t, :, at].astype(F32)
                             + gate[t][:, 0:1] * dot(table[t], answered[t, :, at])).astype(BF16)
        saving = pltpu.make_async_copy(out.at[t], out_h.at[t], save_sem.at[t])
        saving.start()
        saves.append(saving)
    for one in saves:
        one.wait()
    for one in pending + leaving:
        one.wait_send()


def per_device(dp, ex, inbound, queued, routes, gain_a, att_in, att_out, gain_b, router, exp_in, exp_out):
    seq, width = queued.shape[1:]
    k_rows = ex * CAP
    wide = max(k_rows, LANES)
    hid_own = exp_out.shape[2]
    heads_w = att_out.shape[1] * dp
    cols = att_in.shape[2]
    in_rows, out_rows = att_in.shape[1], att_out.shape[1]
    pieces = (max(1, min(4, in_rows // 32)), max(1, min(2, out_rows // 32)))
    n, ny = sum(pieces), max(dp // 2 - 1, 1)
    vm, dma = pltpu.VMEM, pltpu.SemaphoreType.DMA
    dev = dp // 2
    scratch = [
        vm((seq, width), BF16), vm((seq, width), BF16), vm((hid_own, width), BF16), vm((2, seq, width), BF16),
        vm((width, cols), BF16), vm((heads_w, width), BF16), vm((width, hid_own), BF16),
        vm((seq, width), BF16), vm((seq, cols), BF16), vm((seq, heads_w), BF16),
        vm((seq, width), BF16), vm((2, seq, width), BF16), vm((2, seq, k_rows), BF16),
        vm((2, wide, seq), BF16), vm((2, seq, LANES), F32), vm((2, seq, LANES), F32),
        vm((2, wide, width), BF16),
        vm((2, dp, k_rows, width), BF16), vm((dp, k_rows, width), BF16),
        vm((2, dev, k_rows, width), BF16), vm((2, max(dev - 1, 1), k_rows, width), BF16),
        vm((2, k_rows, width), BF16), vm((2, k_rows, width), BF16),
        vm((seq, width), BF16), vm((seq, LANES), F32), vm((k_rows, width), BF16),
        vm((4 * k_rows, hid_own), BF16),
        dma((3,)), dma((3,)), dma((2,)), dma((2,)), dma((2,)),
        *[dma((n, ny))] * 8,
        dma((dp - 1,)), dma((dp - 1,)),
        dma((2, ex - 1)), dma((2, ex - 1)), dma((2, ex, ny)), dma((2, ex, ny)),
        dma((2, ex, dev)), dma((2, ex, dev)), dma((2, dev)), dma((2, dev)),
        dma((2, ex, ny)), dma((2, ex, ny)), dma((2, ex - 1)), dma((2, ex - 1)),
        dma((2 + ex,)), dma((2 + ex,)),
    ]
    here, hbm = pl.BlockSpec(memory_space=pltpu.VMEM), pl.BlockSpec(memory_space=pl.ANY)
    result = pl.pallas_call(
        functools.partial(kernel, dp, ex, pieces),
        out_shape=jax.ShapeDtypeStruct((2, seq, width), BF16),
        in_specs=[hbm, hbm, here, here, hbm, hbm, here, here, hbm, hbm],
        out_specs=hbm,
        scratch_shapes=scratch,
        compiler_params=pltpu.CompilerParams(
            collective_id=0, has_side_effects=True, vmem_limit_bytes=60 * 2**20
        ),
    )(
        inbound[0, 0], queued[0], routes[0, :, 0, :, 0], gain_a, att_in[0], att_out[0], gain_b,
        router[0].T, exp_in[0, 0], exp_out[0, 0],
    )
    return result[None, :, None]


def solution(mesh):
    in_specs = (
        P("section", ("dp", "expert"), None, None),
        P(("dp", "expert"), None, None),
        P("section", None, ("dp", "expert"), None, None),
        P("section", None),
        P("section", "dp", None),
        P("section", "dp", None),
        P("section", None),
        P("section", None, None),
        P("section", "expert", "dp", None),
        P("section", "expert", "dp", None),
    )
    out_specs = P("section", None, ("dp", "expert"), None, None)
    return jax.shard_map(
        functools.partial(per_device, mesh.shape["dp"], mesh.shape["expert"]),
        mesh=mesh, in_specs=in_specs, out_specs=out_specs, check_vma=False,
    )
```

```python
import functools

import jax
import jax.numpy as jnp
from jax import lax
from jax.experimental import pallas as pl
from jax.experimental.pallas import tpu as pltpu
from jax.sharding import PartitionSpec as P

HEAD_DIM = 64
CAP = 16
EPSILON = 1e-06
MESH = pl.DeviceIdType.MESH
F32, BF16 = jnp.float32, jnp.bfloat16
LANES = 128


def dot(a, b):
    return jnp.dot(a, b, preferred_element_type=F32)


def rows_of(start, size):
    return pl.ds(pl.multiple_of(start, 16), size)


def kernel(
    dp, ex, pieces,
    inbound_h, queued_h, routes, gain_a, att_in, att_out, gain_b, router, exp_in, exp_out_h,
    out_h,
    inbound, queued, exp_out, out,
    full_in, full_out, w1, normed, qkv, ctx, entering, mixed, table, table_t, onehot, gate, sent,
    rows, partial, near, parts, answer, answered, far_mixed, far_gate, far_ans, hid,
    own_sem, load_sem, save_sem, sib_s, sib_r, y_s, y_r, fz_s, fz_r, fs_s, fs_r, gs_s, gs_r, w_s, w_r,
    z1_s, z1_r, g_s, g_r, h_s, h_r, n_s, n_r, p_s, p_r, z2_s, z2_r, x_s, x_r,
):
    sec, d, e = lax.axis_index("section"), lax.axis_index("dp"), lax.axis_index("expert")
    y, c, half = d // 2, d % 2, e % 2
    ny = dp // 2
    sib, zpal, far = y * 2 + 1 - c, e + 1 - 2 * half, 1 - sec
    seq, width = inbound.shape
    k_rows = ex * CAP
    hid_own = w1.shape[1]
    heads_w = full_out.shape[0]
    in_rows, out_rows = att_in.shape[0], att_out.shape[0]

    def copy(src, dst, s_sem, r_sem, to):
        return pltpu.make_async_remote_copy(
            src_ref=src, dst_ref=dst, send_sem=s_sem, recv_sem=r_sem,
            device_id=to, device_id_type=MESH,
        )

    loads = []
    for i, (a, b) in enumerate(((inbound_h, inbound), (queued_h, queued), (exp_out_h, exp_out))):
        loads.append(pltpu.make_async_copy(a, b, load_sem.at[i]))
    loads[0].start()
    barrier = pltpu.get_barrier_semaphore()
    for k in range(1, dp):
        pl.semaphore_signal(barrier, inc=1, device_id={"dp": lax.rem(d + k, dp)}, device_id_type=MESH)
    for k in range(1, ex):
        pl.semaphore_signal(barrier, inc=1, device_id={"expert": lax.rem(e + k, ex)}, device_id_type=MESH)
    pl.semaphore_signal(barrier, inc=1, device_id={"section": far}, device_id_type=MESH)
    pl.semaphore_wait(barrier, dp + ex - 1)

    pending = []

    def send(*a):
        one = copy(*a)
        one.start()
        pending.append(one)

    leaving = []

    def leave(*a):
        one = copy(*a)
        one.start()
        leaving.append(one)

    weights = ((0, att_in, full_in, in_rows, pieces[0]), (1, att_out, full_out, out_rows, pieces[1]))
    chunk_list = []
    base = 0
    for which, src, dst, n, cuts in weights:
        size = n // 2 // cuts
        for i in range(cuts):
            chunk_list.append((base + i, src, dst, n, size, i))
        base += cuts
    for idx, src, dst, n, size, i in chunk_list:
        for k in range(1, ny):
            there = lax.rem(y + k, ny) * 2 + c
            off = half * (n // 2) + i * size
            send(src.at[rows_of(off, size)], dst.at[rows_of(d * n + off, size)],
                 y_s.at[idx, k - 1], y_r.at[idx, k - 1], {"dp": there})
    own = []
    for which, src, dst, n, cuts in weights:
        send(src, dst.at[rows_of(d * n, n)], sib_s.at[which], sib_r.at[which], {"dp": sib})
        here = pltpu.make_async_copy(src, dst.at[rows_of(d * n, n)], own_sem.at[which])
        here.start()
        own.append(here)
    w_rows = exp_in.shape[0]
    here = pltpu.make_async_copy(
        exp_in.at[:, pl.ds(pl.multiple_of(d * hid_own, LANES), hid_own)],
        w1.at[rows_of(d * w_rows, w_rows)], own_sem.at[2])
    here.start()
    own.append(here)

    loads[1].start()
    loads[2].start()

    lane = lax.broadcasted_iota(jnp.int32, (seq, LANES), 1)
    wide = table_t.shape[1]
    slots = lax.broadcasted_iota(jnp.int32, (seq, wide), 1)
    earlier = (lax.broadcasted_iota(jnp.int32, (seq, seq), 0)
               > lax.broadcasted_iota(jnp.int32, (seq, seq), 1)).astype(F32).astype(BF16)
    slot_of = []
    for t in range(2):
        chosen = jnp.broadcast_to(routes[t:t + 1, :].astype(F32), (LANES, seq)).T
        hot = (lane.astype(F32) == chosen).astype(F32)
        place = jnp.sum(dot(earlier, hot.astype(BF16)) * hot, axis=1, keepdims=True)
        slot = jnp.where(place < CAP, chosen[:, :1] * CAP + place, -1.0)
        full = (slots.astype(F32) == slot).astype(F32)
        table[t] = full[:, :k_rows].astype(BF16)
        table_t[t] = full.T.astype(BF16)
        onehot[t] = hot
        slot_of.append(slot)

    def norm(src, gain):
        step = 32

        def body(i, _):
            at = pl.ds(pl.multiple_of(i * step, step), step)
            v = src[at, :].astype(F32)
            centre = v - jnp.mean(v, axis=-1, keepdims=True)
            spread = jnp.mean(centre * centre, axis=-1, keepdims=True)
            normed[at, :] = (centre * lax.rsqrt(spread + EPSILON) * gain[...]).astype(BF16)
            return 0

        lax.fori_loop(0, seq // step, body, 0, unroll=True)

    loads[0].wait()
    norm(inbound, gain_a)

    for idx, src, dst, n, size, i in chunk_list:
        for k in range(1, ny):
            come = lax.rem(y - k + ny, ny) * 2 + c
            view = dst.at[rows_of(come * n + half * (n // 2) + i * size, size)]
            copy(view, view, y_s.at[idx, k - 1], y_r.at[idx, k - 1], {"dp": come}).wait_recv()
            send(view, view, fz_s.at[idx, k - 1], fz_r.at[idx, k - 1], {"expert": zpal})
            send(view, view, fs_s.at[idx, k - 1], fs_r.at[idx, k - 1], {"dp": sib})
    for k in range(1, dp):
        to = lax.rem(d + k, dp)
        send(exp_in.at[:, pl.ds(pl.multiple_of(to * hid_own, LANES), hid_own)],
             w1.at[rows_of(d * w_rows, w_rows)], w_s.at[k - 1], w_r.at[k - 1], {"dp": to})
    for idx, src, dst, n, size, i in chunk_list:
        for k in range(1, ny):
            come = lax.rem(y - k + ny, ny) * 2 + c
            view = dst.at[rows_of(come * n + (1 - half) * (n // 2) + i * size, size)]
            copy(view, view, fz_s.at[idx, k - 1], fz_r.at[idx, k - 1], {"expert": zpal}).wait_recv()
            send(view, view, gs_s.at[idx, k - 1], gs_r.at[idx, k - 1], {"dp": sib})

    def land(which):
        _, src, dst, n, cuts = weights[which]
        own[which].wait()
        view = dst.at[rows_of(sib * n, n)]
        copy(view, view, sib_s.at[which], sib_r.at[which], {"dp": sib}).wait_recv()
        for idx, _, to, n, size, i in chunk_list:
            if to is not dst:
                continue
            for k in range(1, ny):
                come = lax.rem(y - k + ny, ny) * 2 + 1 - c
                view = dst.at[rows_of(come * n + half * (n // 2) + i * size, size)]
                copy(view, view, fs_s.at[idx, k - 1], fs_r.at[idx, k - 1], {"dp": sib}).wait_recv()
                view = dst.at[rows_of(come * n + (1 - half) * (n // 2) + i * size, size)]
                copy(view, view, gs_s.at[idx, k - 1], gs_r.at[idx, k - 1], {"dp": sib}).wait_recv()

    far_views = [far_mixed, far_gate]
    for k in range(ex):
        far_views.append(far_ans.at[rows_of(lax.rem(e - k + ex, ex) * CAP, CAP)])
    low = lax.broadcasted_iota(jnp.int32, (seq, LANES), 1) < HEAD_DIM

    saves = []
    for t in range(2):
        if t == 0:
            source = inbound
            land(0)
        else:
            source = entering
            loads[1].wait()
            for i, view in enumerate(far_views[:2]):
                copy(view, view, x_s.at[i], x_r.at[i], {"section": far}).wait_recv()
            far_table = (slots.astype(F32) == far_gate[:, 1:2]).astype(F32)[:, :k_rows].astype(BF16)
            for i, view in enumerate(far_views[2:]):
                copy(view, view, x_s.at[2 + i], x_r.at[2 + i], {"section": far}).wait_recv()
            for j in range(0, width, 256):
                at = slice(j, j + 256)
                came = (far_mixed[:, at].astype(F32)
                        + far_gate[:, 0:1] * dot(far_table, far_ans[:, at]))
                entering[:, at] = jnp.where(sec == 0, queued[:, at].astype(F32), came).astype(BF16)
            norm(entering, gain_a)
        for j in range(0, 3 * heads_w, 256):
            qkv[:, j:j + 256] = dot(normed[...], full_in[:, j:j + 256]).astype(BF16)
        for j in range(0, heads_w, LANES):
            q = qkv[:, j:j + LANES] * jnp.asarray(HEAD_DIM ** -0.5, BF16)
            key = qkv[:, heads_w + j:heads_w + j + LANES]
            val = qkv[:, 2 * heads_w + j:2 * heads_w + j + LANES]
            both = []
            for mask in (low, jnp.logical_not(low)):
                one = jnp.where(mask, q.astype(F32), 0.0).astype(BF16)
                s = lax.dot_general(one, key, (((1,), (1,)), ((), ())), preferred_element_type=F32)
                w = jnp.exp(s - jnp.max(s, axis=1, keepdims=True))
                both.append(dot(w.astype(BF16), val) / jnp.sum(w, axis=1, keepdims=True))
            ctx[:, j:j + LANES] = jnp.where(low, both[0], both[1]).astype(BF16)
        if t == 0:
            land(1)
        for j in range(0, width, 256):
            at = slice(j, j + 256)
            mixed[t, :, at] = (source[:, at].astype(F32) + dot(ctx[...], full_out[:, at])).astype(BF16)
        if t == 0:
            send(mixed.at[0], far_mixed, x_s.at[0], x_r.at[0], {"section": far})
        norm(mixed.at[t], gain_b)
        for j in range(0, width, 256):
            at = slice(j, j + 256)
            sent[t, :, at] = dot(table_t[t], normed[:, at])[:].astype(BF16)
        for k in range(1, ex):
            to = lax.rem(e + k, ex)
            send(sent.at[t, rows_of(to * CAP, CAP)], rows.at[t, d, rows_of(e * CAP, CAP)],
                 z1_s.at[t, k - 1], z1_r.at[t, k - 1], {"expert": to})
        rows[t, d, rows_of(e * CAP, CAP), :] = sent[t, rows_of(e * CAP, CAP), :]
        logits = lax.dot_general(normed[...], router[...], (((1,), (1,)), ((), ())), preferred_element_type=F32)
        picked = jnp.sum(logits * onehot[t][:, :ex], axis=1, keepdims=True)
        gating = 1.0 / (1.0 + jnp.exp(-picked))
        gate[t] = jnp.where(lane == 0, gating, jnp.where(lane == 1, slot_of[t], 0.0))
        if t == 0:
            send(gate.at[0], far_gate, x_s.at[1], x_r.at[1], {"section": far})
        def pass_on(kk):
            at = rows_of(lax.rem(e - kk + ex, ex) * CAP, CAP)
            for k in range(1, ny):
                come = lax.rem(y - k + ny, ny) * 2 + c
                view = rows.at[t, come, at]
                copy(view, view, g_s.at[t, kk, k - 1], g_r.at[t, kk, k - 1], {"dp": come}).wait_recv()

        for kk in range(ex):
            come = lax.rem(e - kk + ex, ex)
            view = rows.at[t, d, rows_of(come * CAP, CAP)]
            if kk > 0:
                copy(view, view, z1_s.at[t, kk - 1], z1_r.at[t, kk - 1], {"expert": come}).wait_recv()
            for k in range(1, ny):
                send(view, view, g_s.at[t, kk, k - 1], g_r.at[t, kk, k - 1],
                     {"dp": lax.rem(y + k, ny) * 2 + c})
                send(view, view, h_s.at[t, kk, k], h_r.at[t, kk, k],
                     {"dp": lax.rem(y + k, ny) * 2 + 1 - c})
            send(view, view, h_s.at[t, kk, 0], h_r.at[t, kk, 0], {"dp": sib})
        for kk in range(ex):
            pass_on(kk)
        if t == 0:
            own[2].wait()
            loads[2].wait()
            for k in range(1, dp):
                come = lax.rem(d - k + dp, dp)
                view = w1.at[rows_of(come * w_rows, w_rows)]
                copy(view, view, w_s.at[k - 1], w_r.at[k - 1], {"dp": come}).wait_recv()
        for kk in range(ex):
            at = rows_of(lax.rem(e - kk + ex, ex) * CAP, CAP)
            for k in range(ny):
                view = rows.at[t, lax.rem(y - k + ny, ny) * 2 + 1 - c, at]
                copy(view, view, h_s.at[t, kk, k], h_r.at[t, kk, k], {"dp": sib}).wait_recv()

        group = 4

        def experts(i, _):
            at = pl.ds(i * group, group)
            x = rows[t, at].reshape(group * k_rows, width)
            for j in range(0, hid_own, 128):
                h = dot(x, w1[:, j:j + 128])
                h = 0.5 * h * (1.0 + lax.erf(h * 0.7071067811865476))
                hid[:, j:j + 128] = h.astype(BF16)
            for j in range(0, width, 256):
                a = dot(hid[...], exp_out[:, j:j + 256]).astype(BF16)
                partial[at, :, j:j + 256] = a.reshape(group, k_rows, 256)
            return 0

        for one in leaving:
            one.wait_send()
        leaving.clear()
        lax.fori_loop(0, dp // group, experts, 0)
        for k in (*range(1, ny), 0):
            to = lax.rem(y + k, ny) * 2
            leave(partial.at[to + 1 - c], near.at[t, k], n_s.at[t, k], n_r.at[t, k], {"dp": sib})
        for k in range(1, ny):
            to = lax.rem(y + k, ny) * 2 + c
            view = near.at[t, k]
            copy(view, view, n_s.at[t, k], n_r.at[t, k], {"dp": sib}).wait_recv()
            for kk in (*range(1, ex), 0):
                at = rows_of(lax.rem(e + kk, ex) * CAP, CAP)
                partial[to, at, :] = (partial[to, at, :].astype(F32) + near[t, k, at, :].astype(F32)).astype(BF16)
                leave(partial.at[to, at], parts.at[t, k - 1, at],
                      p_s.at[t, kk, k - 1], p_r.at[t, kk, k - 1], {"dp": to})
        view = near.at[t, 0]
        copy(view, view, n_s.at[t, 0], n_r.at[t, 0], {"dp": sib}).wait_recv()
        for kk in (*range(1, ex), 0):
            to = lax.rem(e + kk, ex)
            at = rows_of(to * CAP, CAP)
            total = partial[d, at, :].astype(F32) + near[t, 0, at, :].astype(F32)
            for k in range(1, ny):
                view = parts.at[t, k - 1, at]
                copy(view, view, p_s.at[t, kk, k - 1], p_r.at[t, kk, k - 1],
                     {"dp": lax.rem(y - k + ny, ny) * 2 + c}).wait_recv()
                total += parts[t, k - 1, at, :].astype(F32)
            if kk > 0:
                answer[t, at, :] = total.astype(BF16)
                send(answer.at[t, at], answered.at[t, rows_of(e * CAP, CAP)],
                     z2_s.at[t, kk - 1], z2_r.at[t, kk - 1], {"expert": to})
            else:
                answered[t, at, :] = total.astype(BF16)
        for kk in range(ex):
            come = lax.rem(e - kk + ex, ex)
            view = answered.at[t, rows_of(come * CAP, CAP)]
            if kk > 0:
                copy(view, view, z2_s.at[t, kk - 1], z2_r.at[t, kk - 1], {"expert": come}).wait_recv()
            if t == 0:
                send(view, far_views[2 + kk], x_s.at[2 + kk], x_r.at[2 + kk], {"section": far})
        for j in range(0, width, 256):
            at = slice(j, j + 256)
            out[t, :, at] = (mixed[t, :, at].astype(F32)
                             + gate[t][:, 0:1] * dot(table[t], answered[t, :, at])).astype(BF16)
        saving = pltpu.make_async_copy(out.at[t], out_h.at[t], save_sem.at[t])
        saving.start()
        saves.append(saving)
    for one in saves:
        one.wait()
    for one in pending + leaving:
        one.wait_send()


def per_device(dp, ex, inbound, queued, routes, gain_a, att_in, att_out, gain_b, router, exp_in, exp_out):
    seq, width = queued.shape[1:]
    k_rows = ex * CAP
    wide = max(k_rows, LANES)
    hid_own = exp_out.shape[2]
    heads_w = att_out.shape[1] * dp
    cols = att_in.shape[2]
    in_rows, out_rows = att_in.shape[1], att_out.shape[1]
    pieces = (max(1, min(8, in_rows // 32)), max(1, min(4, out_rows // 32)))
    n, ny = sum(pieces), max(dp // 2 - 1, 1)
    vm, dma = pltpu.VMEM, pltpu.SemaphoreType.DMA
    dev = dp // 2
    scratch = [
        vm((seq, width), BF16), vm((seq, width), BF16), vm((hid_own, width), BF16), vm((2, seq, width), BF16),
        vm((width, cols), BF16), vm((heads_w, width), BF16), vm((width, hid_own), BF16),
        vm((seq, width), BF16), vm((seq, cols), BF16), vm((seq, heads_w), BF16),
        vm((seq, width), BF16), vm((2, seq, width), BF16), vm((2, seq, k_rows), BF16),
        vm((2, wide, seq), BF16), vm((2, seq, LANES), F32), vm((2, seq, LANES), F32),
        vm((2, wide, width), BF16),
        vm((2, dp, k_rows, width), BF16), vm((dp, k_rows, width), BF16),
        vm((2, dev, k_rows, width), BF16), vm((2, max(dev - 1, 1), k_rows, width), BF16),
        vm((2, k_rows, width), BF16), vm((2, k_rows, width), BF16),
        vm((seq, width), BF16), vm((seq, LANES), F32), vm((k_rows, width), BF16),
        vm((4 * k_rows, hid_own), BF16),
        dma((3,)), dma((3,)), dma((2,)), dma((2,)), dma((2,)),
        *[dma((n, ny))] * 8,
        dma((dp - 1,)), dma((dp - 1,)),
        dma((2, ex - 1)), dma((2, ex - 1)), dma((2, ex, ny)), dma((2, ex, ny)),
        dma((2, ex, dev)), dma((2, ex, dev)), dma((2, dev)), dma((2, dev)),
        dma((2, ex, ny)), dma((2, ex, ny)), dma((2, ex - 1)), dma((2, ex - 1)),
        dma((2 + ex,)), dma((2 + ex,)),
    ]
    here, hbm = pl.BlockSpec(memory_space=pltpu.VMEM), pl.BlockSpec(memory_space=pl.ANY)
    result = pl.pallas_call(
        functools.partial(kernel, dp, ex, pieces),
        out_shape=jax.ShapeDtypeStruct((2, seq, width), BF16),
        in_specs=[hbm, hbm, here, here, hbm, hbm, here, here, hbm, hbm],
        out_specs=hbm,
        scratch_shapes=scratch,
        compiler_params=pltpu.CompilerParams(
            collective_id=0, has_side_effects=True, vmem_limit_bytes=60 * 2**20
        ),
    )(
        inbound[0, 0], queued[0], routes[0, :, 0, :, 0], gain_a, att_in[0], att_out[0], gain_b,
        router[0].T, exp_in[0, 0], exp_out[0, 0],
    )
    return result[None, :, None]


def solution(mesh):
    in_specs = (
        P("section", ("dp", "expert"), None, None),
        P(("dp", "expert"), None, None),
        P("section", None, ("dp", "expert"), None, None),
        P("section", None),
        P("section", "dp", None),
        P("section", "dp", None),
        P("section", None),
        P("section", None, None),
        P("section", "expert", "dp", None),
        P("section", "expert", "dp", None),
    )
    out_specs = P("section", None, ("dp", "expert"), None, None)
    return jax.shard_map(
        functools.partial(per_device, mesh.shape["dp"], mesh.shape["expert"]),
        mesh=mesh, in_specs=in_specs, out_specs=out_specs, check_vma=False,
    )
```
